256 devices in a mesh: dp: 32 (over z, x), tensor: 8 (over y, core).
Axes of the slice: x: 4, y: 4, z: 8, core: 2. Of those that a mesh axis runs over, the one named last changes fastest.
Arguments:
- layer_input: bfloat16 [8192, 512], P('dp'), may hold values from -6 to 6
- output_grad: bfloat16 [8192, 28672], P('dp', 'tensor'), may hold values from -6 to 6
- feedback: bfloat16 [16384, 28672], P('dp', 'tensor'), may hold values from -6 to 6
- basis_prev: float32 [64, 28672], P(None, 'tensor'), may hold values from -6 to 6
Outputs:
- factor_left: float32 [64, 512], replicated
- basis_next: float32 [64, 28672], P(None, 'tensor')
- feedback_next: bfloat16 [16384, 28672], P('dp', 'tensor')
The draws below stay inside these ranges and needn't reach their ends.
All inputs are finite; a program needn't handle non-finite values.
Results may differ from the reference program's by a relative error of at most 0.0065.
Values sent between devices are 32-bit elements; how exact they have to be, the bound alone decides.
No kernel may reach another device: no remote copies, remote signals or barrier semaphores. Data moves between devices by JAX's collectives and lax.ppermute only.
A program may use at most 64 MiB of HBM per device.

```python
import math
import jax
import jax.numpy as jnp
from jax import lax

FF = 28672
RANK = 64
ROWS = 512
TOK_DEV = 256
TOKENS = 8192
FEED_ROWS = 16384
N_DP = 32


def level_of(rng, shape, split, low, top_value):
    loudness = 1.0
    for position, shards_of in split:
        heights = jax.random.uniform(jax.random.fold_in(jax.random.fold_in(rng, 6), position), (shards_of,), jnp.float32, low / len(split), top_value / len(split))
        loudness = loudness * jnp.repeat(jnp.exp(heights), shape[position] // shards_of).reshape((-1,) + (1,) * (len(shape) - 1 - position))
    return loudness


def gaussian(stream_key, shape, deviation, reach, shards=(), kind=jnp.bfloat16):
    loudness = level_of(stream_key, shape, shards, -0.22, 0.18) if shards else 1.0
    values = jax.random.normal(stream_key, shape, jnp.float32) * deviation * loudness
    return jnp.minimum(jnp.maximum(values, -reach), reach).astype(kind)


def setup_inputs(seed: int = 0) -> dict:
    keys = jax.random.split(jax.random.key(seed), 5)
    layer_input = gaussian(keys[0], (TOKENS, ROWS), 1.0, 6.0, ((0, 32),))
    output_grad = gaussian(keys[1], (TOKENS, FF), 1.0, 6.0, ((0, 32), (1, 8)))
    feedback = gaussian(keys[2], (FEED_ROWS, FF), 0.7, 6.0, ((0, 32), (1, 8)))
    basis_prev = gaussian(keys[3], (RANK, FF), 1.0, 6.0, ((1, 8),), jnp.float32)
    return dict(layer_input=layer_input, output_grad=output_grad, feedback=feedback, basis_prev=basis_prev)


def orthonormal(factor_sum):
    gram_matrix = jnp.dot(factor_sum, factor_sum.T, precision=lax.Precision.HIGHEST)
    lower_factor = jnp.linalg.cholesky(gram_matrix)
    return jax.scipy.linalg.solve_triangular(lower_factor, factor_sum, lower=True)

def corrected_for(layer_input, output_grad, feedback, replica):
    inputs_r = lax.dynamic_slice_in_dim(layer_input, (replica * TOK_DEV).astype(jnp.int32), TOK_DEV, 0)
    grads_r = lax.dynamic_slice_in_dim(output_grad, (replica * TOK_DEV).astype(jnp.int32), TOK_DEV, 0)
    buffer_r = lax.dynamic_slice_in_dim(feedback, (replica * ROWS).astype(jnp.int32), ROWS, 0)
    weight_grad = lax.dot_general(inputs_r.astype(jnp.float32), grads_r.astype(jnp.float32), (((0,), (0,)), ((), ())), preferred_element_type=jnp.float32)
    weight_grad = weight_grad * (1.0 / math.sqrt(TOK_DEV))
    return (weight_grad + buffer_r.astype(jnp.float32)).astype(jnp.bfloat16)

def reference(layer_input, output_grad, feedback, basis_prev):
    basis_low = basis_prev.astype(jnp.bfloat16)
    replicas = jnp.arange(N_DP, dtype=jnp.int32)

    def factor_step(total, replica):
        corrected = corrected_for(layer_input, output_grad, feedback, replica)
        term = lax.dot_general(basis_low.astype(jnp.float32), corrected.astype(jnp.float32), (((1,), (1,)), ((), ())), preferred_element_type=jnp.float32)
        return (total + term, None)
    factor_sum, _ = lax.scan(factor_step, jnp.zeros((RANK, ROWS), jnp.float32), replicas)
    factor_left = orthonormal(factor_sum)
    factor_low = factor_left.astype(jnp.bfloat16)

    def basis_step(total, replica):
        corrected = corrected_for(layer_input, output_grad, feedback, replica)
        return (total + jnp.dot(factor_low.astype(jnp.float32), corrected.astype(jnp.float32), preferred_element_type=jnp.float32), None)
    basis_total, _ = lax.scan(basis_step, jnp.zeros((RANK, FF), jnp.float32), replicas)
    basis_next = basis_total / N_DP
    basis_round = basis_next.astype(jnp.bfloat16)

    def feedback_for(replica):
        corrected = corrected_for(layer_input, output_grad, feedback, replica)
        approx = lax.dot_general(factor_low.astype(jnp.float32), basis_round.astype(jnp.float32), (((0,), (0,)), ((), ())), preferred_element_type=jnp.float32)
        return (corrected.astype(jnp.float32) - approx).astype(jnp.bfloat16)
    feedback_next = lax.map(feedback_for, replicas).reshape(N_DP * ROWS, FF)
    return (factor_left, basis_next, feedback_next)
```

```python
import math

import jax
import jax.numpy as jnp
from jax import lax
from jax.sharding import Mesh
from jax.sharding import PartitionSpec as P

SIZES = dict(z=8, x=4, y=4, c=2)
PLANE = ("x", "y", "c")


def group_size(axes):
    return math.prod(SIZES[a] for a in axes)


def shift(block, axis, step):
    n = SIZES[axis]
    return lax.ppermute(block, axis, [(i, (i + step) % n) for i in range(n)])


def scatter_sum_direct(rows, axes):
    n = group_size(axes)
    parts = lax.all_to_all(rows, axes, 0, 0, tiled=True)
    return jnp.sum(parts.reshape((n, rows.shape[0] // n) + rows.shape[1:]), 0)


def copies(block, axes):
    n = group_size(axes)
    sent = jnp.broadcast_to(block[None], (n,) + block.shape)
    return lax.all_to_all(sent, axes, 0, 0, tiled=True)


def gather_direct(block, axes):
    return copies(block, axes).reshape((-1,) + block.shape[1:])


def scatter_sum_ring(rows, axis):
    n = SIZES[axis]
    height = rows.shape[0] // n
    me = lax.axis_index(axis)
    arrived = [
        shift(lax.dynamic_slice_in_dim(rows, lax.rem(me + k, n) * height, height, 0), axis, k)
        for k in range(1, n)
    ]
    return lax.dynamic_slice_in_dim(rows, me * height, height, 0) + sum(arrived)


def gather_ring(block, axis):
    n = SIZES[axis]
    height = block.shape[0]
    me = lax.axis_index(axis)
    out = jnp.zeros((height * n,) + block.shape[1:], block.dtype)
    for k in range(n):
        arrived = shift(block, axis, k) if k else block
        out = lax.dynamic_update_slice_in_dim(out, arrived, lax.rem(me - k + n, n) * height, 0)
    return out


def sum_all(factor_part):
    rows = factor_part.reshape(256, 128)
    piece = scatter_sum_direct(rows, PLANE)
    piece = jnp.sum(copies(piece, ("z",)), 0)
    return gather_direct(piece, PLANE).reshape(factor_part.shape)


def sum_dp(basis_term):
    rows = basis_term.reshape(224, 1024)
    piece = scatter_sum_ring(rows, "x")
    piece = scatter_sum_direct(piece, ("z",))
    piece = gather_direct(piece, ("z",))
    return gather_ring(piece, "x").reshape(basis_term.shape)


def cholesky_solve(gram_matrix, columns):
    lower_factor = jnp.linalg.cholesky(gram_matrix)
    return jax.scipy.linalg.solve_triangular(lower_factor, columns, lower=True)


def local(layer_input, output_grad, feedback, basis_prev):
    token_count = layer_input.shape[0]
    weight_grad = lax.dot_general(
        layer_input, output_grad, (((0,), (0,)), ((), ())), preferred_element_type=jnp.float32
    )
    weight_grad = weight_grad * (1.0 / math.sqrt(token_count))
    corrected = (weight_grad + feedback.astype(jnp.float32)).astype(jnp.bfloat16)
    basis_low = basis_prev.astype(jnp.bfloat16)
    factor_part = lax.dot_general(
        basis_low, corrected, (((1,), (1,)), ((), ())), preferred_element_type=jnp.float32
    )
    factor_sum = sum_all(factor_part)
    gram_matrix = jnp.dot(factor_sum, factor_sum.T, precision=lax.Precision.HIGHEST)
    factor_left = cholesky_solve(gram_matrix, factor_sum)
    factor_low = factor_left.astype(jnp.bfloat16)
    basis_term = jnp.dot(factor_low, corrected, preferred_element_type=jnp.float32)
    basis_next = sum_dp(basis_term) / (SIZES["z"] * SIZES["x"])
    basis_round = basis_next.astype(jnp.bfloat16)
    approx = lax.dot_general(
        factor_low, basis_round, (((0,), (0,)), ((), ())), preferred_element_type=jnp.float32
    )
    feedback_next = (corrected.astype(jnp.float32) - approx).astype(jnp.bfloat16)
    return (factor_left, basis_next, feedback_next)


def solution(mesh):
    fine = Mesh(mesh.devices.reshape(8, 4, 4, 2), ("z", "x", "y", "c"))
    dp, tensor = ("z", "x"), ("y", "c")
    in_specs = (P(dp, None), P(dp, tensor), P(dp, tensor), P(None, tensor))
    out_specs = (P(), P(None, tensor), P(dp, tensor))
    return jax.shard_map(local, mesh=fine, in_specs=in_specs, out_specs=out_specs, check_vma=False)
```

```python
import functools
import math

import jax
import jax.numpy as jnp
from jax import lax
from jax.experimental import pallas as pl
from jax.experimental.pallas import tpu as pltpu
from jax.sharding import Mesh
from jax.sharding import PartitionSpec as P

SIZES = dict(z=8, x=4, y=4, c=2)
PLANE = ("x", "y", "c")
REPLICAS = SIZES["z"] * SIZES["x"]
QUARTERS = SIZES["x"]
VMEM = pltpu.CompilerParams(vmem_limit_bytes=32 << 20)


def shift(block, axis, step):
    n = SIZES[axis]
    return lax.ppermute(block, axis, [(i, (i + step) % n) for i in range(n)])


def copies(block, axes):
    n = math.prod(SIZES[a] for a in axes)
    sent = jnp.broadcast_to(block[None], (n,) + block.shape)
    return lax.all_to_all(sent, axes, 0, 0, tiled=True)


def sum_all(tiles):
    piece = jnp.sum(lax.all_to_all(tiles, PLANE, 0, 0, tiled=True), 0)
    piece = jnp.sum(copies(piece, ("z",)), 0)
    return copies(piece, PLANE)


def corrected_kernel(x_ref, g_ref, fb_ref, basis_ref, corrected_ref, tiles_ref, xt_ref, acc_ref):
    step = pl.program_id(0)

    @pl.when(step == 0)
    def _():
        xt_ref[...] = x_ref[...].T
        acc_ref[...] = jnp.zeros_like(acc_ref)

    grad = jnp.dot(xt_ref[...], g_ref[...], preferred_element_type=jnp.float32)
    grad = grad * (1.0 / math.sqrt(x_ref.shape[0])) + fb_ref[...].astype(jnp.float32)
    corrected = grad.astype(jnp.bfloat16)
    corrected_ref[0] = corrected
    acc_ref[...] += lax.dot_general(
        basis_ref[...].astype(jnp.bfloat16),
        corrected,
        (((1,), (1,)), ((), ())),
        preferred_element_type=jnp.float32,
    )

    @pl.when(step == pl.num_programs(0) - 1)
    def _():
        rows, columns = acc_ref.shape
        for i in range(rows // 8):
            for j in range(columns // 128):
                tiles_ref[i * (columns // 128) + j] = acc_ref[8 * i : 8 * i + 8, 128 * j : 128 * j + 128]


def corrected_and_factor(layer_input, output_grad, feedback, basis_prev):
    tokens, rows = layer_input.shape
    columns, rank = output_grad.shape[1], basis_prev.shape[0]
    width = columns // QUARTERS
    return pl.pallas_call(
        corrected_kernel,
        grid=(QUARTERS,),
        in_specs=[
            pl.BlockSpec((tokens, rows), lambda q: (0, 0)),
            pl.BlockSpec((tokens, width), lambda q: (0, q)),
            pl.BlockSpec((rows, width), lambda q: (0, q)),
            pl.BlockSpec((rank, width), lambda q: (0, q)),
        ],
        out_specs=[
            pl.BlockSpec((1, rows, width), lambda q: (q, 0, 0)),
            pl.BlockSpec((rank * rows // 1024, 8, 128), lambda q: (0, 0, 0)),
        ],
        out_shape=[
            jax.ShapeDtypeStruct((QUARTERS, rows, width), jnp.bfloat16),
            jax.ShapeDtypeStruct((rank * rows // 1024, 8, 128), jnp.float32),
        ],
        scratch_shapes=[
            pltpu.VMEM((rows, tokens), jnp.bfloat16),
            pltpu.VMEM((rank, rows), jnp.float32),
        ],
        compiler_params=VMEM,
        name="corrected",
    )(layer_input, output_grad, feedback, basis_prev)


def eliminate(factor):
    rank, columns = factor.shape
    both = jnp.concatenate([factor, factor], 0)
    gram = lax.dot_general(
        factor,
        both,
        (((1,), (1,)), ((), ())),
        preferred_element_type=jnp.float32,
        precision=lax.Precision.HIGHEST,
    )
    blocks = rank // 8
    lanes = columns // 128
    table = [
        [gram[8 * i : 8 * i + 8]]
        + [factor[8 * i : 8 * i + 8, 128 * j : 128 * j + 128] for j in range(lanes)]
        for i in range(blocks)
    ]
    sublane = lax.broadcasted_iota(jnp.int32, (8, 128), 0)
    spread = lambda row: jnp.broadcast_to(row, (8, 128))
    out = []
    for p in range(blocks):
        below = range(p, blocks)
        col = [
            {i: jnp.broadcast_to(table[i][0][:, 8 * p + j : 8 * p + j + 1], (8, 128)) for i in below}
            for j in range(8)
        ]
        pivots = jnp.ones((8, 128), jnp.float32)
        for j in range(8):
            pivot = spread(col[j][p][j : j + 1])
            pivots = jnp.where(sublane == j, pivot, pivots)
            if p == blocks - 1 and j == 7:
                break
            inverse = 1.0 / pivot
            mult = {i: col[j][i] * inverse for i in below}
            mult[p] = jnp.where(sublane > j, mult[p], 0.0)
            for k in range(j + 1, 8):
                entry = spread(col[j][p][k : k + 1])
                for i in below:
                    col[k][i] = col[k][i] - mult[i] * entry
            for t in range(lanes + 1):
                if t == 0 and p == blocks - 1:
                    continue
                row = spread(table[p][t][j : j + 1])
                for i in below:
                    table[i][t] = table[i][t] - mult[i] * row
        scale = lax.rsqrt(pivots)
        out.append([table[p][t] * scale for t in range(1, lanes + 1)])
    return out


def factor_kernel(me_ref, tiles_ref, corrected_hbm, left_ref, low_ref, *rest):
    term_refs, (corrected_ref, sem) = rest[:QUARTERS], rest[QUARTERS:]
    copy = pltpu.make_async_copy(corrected_hbm, corrected_ref, sem)
    copy.start()
    rank, columns = left_ref.shape
    lanes = columns // 128
    factor = jnp.concatenate(
        [
            jnp.concatenate([tiles_ref[i * lanes + j] for j in range(lanes)], 1)
            for i in range(rank // 8)
        ],
        0,
    )
    blocks = eliminate(factor)
    for i, block in enumerate(blocks):
        for j, tile in enumerate(block):
            left_ref[8 * i : 8 * i + 8, 128 * j : 128 * j + 128] = tile
    low = left_ref[...].astype(jnp.bfloat16)
    low_ref[...] = low
    copy.wait()
    me = me_ref[0]
    for k in range(QUARTERS):
        quarter = lax.rem(me + k, QUARTERS)
        term_refs[k][...] = jnp.dot(low, corrected_ref[quarter], preferred_element_type=jnp.float32)


def factor_and_terms(me, tiles, corrected, rank):
    quarters, rows, width = corrected.shape
    whole = pl.BlockSpec(memory_space=pltpu.VMEM)
    return pl.pallas_call(
        factor_kernel,
        in_specs=[
            pl.BlockSpec(memory_space=pltpu.SMEM),
            whole,
            pl.BlockSpec(memory_space=pl.ANY),
        ],
        out_specs=[whole] * (2 + quarters),
        out_shape=[
            jax.ShapeDtypeStruct((rank, rows), jnp.float32),
            jax.ShapeDtypeStruct((rank, rows), jnp.bfloat16),
        ]
        + [jax.ShapeDtypeStruct((rank, width), jnp.float32)] * quarters,
        scratch_shapes=[pltpu.VMEM(corrected.shape, jnp.bfloat16), pltpu.SemaphoreType.DMA(())],
        compiler_params=VMEM,
        name="factor",
    )(me, tiles, corrected)


def feedback_kernel(q_ref, total_ref, low_t_ref, corrected_ref, *rest):
    next_ref, feedback_ref = rest[-2:]
    basis_next = total_ref[...] * (1.0 / REPLICAS)
    next_ref[...] = basis_next
    approx = jnp.dot(
        low_t_ref[...], basis_next.astype(jnp.bfloat16), preferred_element_type=jnp.float32
    )
    feedback_ref[...] = (corrected_ref[0].astype(jnp.float32) - approx).astype(jnp.bfloat16)


def finish_quarter(quarter, total, low_t, corrected, so_far):
    quarters, rows, width = corrected.shape
    rank = total.shape[0]
    return pl.pallas_call(
        feedback_kernel,
        grid_spec=pltpu.PrefetchScalarGridSpec(
            num_scalar_prefetch=1,
            grid=(1,),
            in_specs=[
                pl.BlockSpec((rank, width), lambda s, q: (0, 0)),
                pl.BlockSpec((rows, rank), lambda s, q: (0, 0)),
                pl.BlockSpec((1, rows, width), lambda s, q: (q[0], 0, 0)),
            ]
            + [pl.BlockSpec(memory_space=pl.ANY)] * len(so_far),
            out_specs=[
                pl.BlockSpec((rank, width), lambda s, q: (0, q[0])),
                pl.BlockSpec((rows, width), lambda s, q: (0, q[0])),
            ],
        ),
        out_shape=[
            jax.ShapeDtypeStruct((rank, width * quarters), jnp.float32),
            jax.ShapeDtypeStruct((rows, width * quarters), jnp.bfloat16),
        ],
        input_output_aliases={4: 0, 5: 1} if so_far else {},
        compiler_params=VMEM,
        name="feedback",
    )(quarter, total, low_t, corrected, *so_far)


def local(layer_input, output_grad, feedback, basis_prev):
    me = lax.axis_index("x").reshape(1)
    corrected, tiles = corrected_and_factor(layer_input, output_grad, feedback, basis_prev)
    tiles = sum_all(tiles)
    factor_left, factor_low, *terms = factor_and_terms(me, tiles, corrected, basis_prev.shape[0])
    factor_low_t = factor_low.T

    arrived = [shift(terms[k], "x", k) for k in range(1, QUARTERS)]
    quarter = terms[0] + sum(arrived)
    piece = lax.all_to_all(quarter.reshape(SIZES["z"], 8, -1), "z", 0, 0, tiled=True)
    piece = jnp.sum(piece, 0)
    quarter = copies(piece, ("z",)).reshape(quarter.shape)
    totals = [quarter] + [shift(quarter, "x", k) for k in range(1, QUARTERS)]
    results = ()
    for k in range(QUARTERS):
        owner = lax.rem(me + (QUARTERS - k), QUARTERS)
        results = finish_quarter(owner, totals[k], factor_low_t, corrected, results)
    return (factor_left,) + tuple(results)


def solution(mesh):
    fine = Mesh(mesh.devices.reshape(8, 4, 4, 2), ("z", "x", "y", "c"))
    dp, tensor = ("z", "x"), ("y", "c")
    in_specs = (P(dp, None), P(dp, tensor), P(dp, tensor), P(None, tensor))
    out_specs = (P(), P(None, tensor), P(dp, tensor))
    return jax.shard_map(local, mesh=fine, in_specs=in_specs, out_specs=out_specs, check_vma=False)
```

```python
import functools
import math

import jax
import jax.numpy as jnp
from jax import lax
from jax.experimental import pallas as pl
from jax.experimental.pallas import tpu as pltpu
from jax.sharding import Mesh
from jax.sharding import PartitionSpec as P

SIZES = dict(z=8, x=4, y=4, c=2)
PLANE = ("x", "y", "c")
REPLICAS = SIZES["z"] * SIZES["x"]
QUARTERS = SIZES["x"]
STRIPS = 4
ARRIVING = (0, 1, 3, 2)
VMEM = pltpu.CompilerParams(vmem_limit_bytes=24 << 20)


def in_hbm(*arrays):
    return [pltpu.with_memory_space_constraint(a, pltpu.HBM) for a in arrays]


def in_vmem(*arrays):
    return [pltpu.with_memory_space_constraint(a, pltpu.VMEM) for a in arrays]


def shift(block, axis, step):
    n = SIZES[axis]
    return lax.ppermute(block, axis, [(i, (i + step) % n) for i in range(n)])


def copies(block, axes):
    n = math.prod(SIZES[a] for a in axes)
    sent = jnp.broadcast_to(block[None], (n,) + block.shape)
    return lax.all_to_all(sent, axes, 0, 0, tiled=True)


def sum_all(tiles):
    parts = lax.all_to_all(tiles, PLANE, 0, 0, tiled=True)
    parts = copies(jnp.sum(parts, 0), ("z",))
    return copies(jnp.sum(parts, 0), PLANE)


def corrected_kernel(
    x_hbm, g_hbm, fb_hbm, basis_hbm, corrected_hbm, tiles_ref,
    x_ref, g_ref, fb_ref, basis_ref, out_ref, x_sem, in_sems, out_sems,
):
    width = g_ref.shape[2]
    fetch_x = pltpu.make_async_copy(x_hbm, x_ref, x_sem)
    fetch_x.start()
    fetches = []
    for q in range(QUARTERS):
        columns = pl.ds(q * width, width)
        pairs = ((g_hbm, g_ref), (fb_hbm, fb_ref), (basis_hbm, basis_ref))
        fetches.append(
            [
                pltpu.make_async_copy(whole.at[:, columns], part.at[q], in_sems.at[q, i])
                for i, (whole, part) in enumerate(pairs)
            ]
        )
        for fetch in fetches[q]:
            fetch.start()
    fetch_x.wait()
    xt = x_ref[...].T

    def factor_part(q):
        return lax.dot_general(
            basis_ref[q].astype(jnp.bfloat16),
            out_ref[q],
            (((1,), (1,)), ((), ())),
            preferred_element_type=jnp.float32,
        )

    parts = []
    stores = []
    for q in range(QUARTERS):
        for fetch in fetches[q]:
            fetch.wait()
        grad = jnp.dot(xt, g_ref[q], preferred_element_type=jnp.float32)
        if q:
            parts.append(factor_part(q - 1))
        grad = grad * (1.0 / math.sqrt(x_ref.shape[0])) + fb_ref[q].astype(jnp.float32)
        out_ref[q] = grad.astype(jnp.bfloat16)
        stores.append(pltpu.make_async_copy(out_ref.at[q], corrected_hbm.at[q], out_sems.at[q]))
        stores[q].start()
    parts.append(factor_part(QUARTERS - 1))
    total = sum(parts[1:], parts[0])
    rows, columns = total.shape
    for i in range(rows // 8):
        for j in range(columns // 128):
            tiles_ref[i * (columns // 128) + j] = total[8 * i : 8 * i + 8, 128 * j : 128 * j + 128]
    for store in stores:
        store.wait()


def corrected_and_factor(layer_input, output_grad, feedback, basis_prev):
    tokens, rows = layer_input.shape
    columns, rank = output_grad.shape[1], basis_prev.shape[0]
    width = columns // QUARTERS
    return pl.pallas_call(
        corrected_kernel,
        in_specs=[pl.BlockSpec(memory_space=pltpu.HBM)] * 4,
        out_specs=[pl.BlockSpec(memory_space=pltpu.HBM), pl.BlockSpec(memory_space=pltpu.VMEM)],
        out_shape=[
            pltpu.HBM((QUARTERS, rows, width), jnp.bfloat16),
            jax.ShapeDtypeStruct((rank * rows // 1024, 8, 128), jnp.float32),
        ],
        scratch_shapes=[
            pltpu.VMEM((tokens, rows), jnp.bfloat16),
            pltpu.VMEM((QUARTERS, tokens, width), jnp.bfloat16),
            pltpu.VMEM((QUARTERS, rows, width), jnp.bfloat16),
            pltpu.VMEM((QUARTERS, rank, width), jnp.float32),
            pltpu.VMEM((QUARTERS, rows, width), jnp.bfloat16),
            pltpu.SemaphoreType.DMA(()),
            pltpu.SemaphoreType.DMA((QUARTERS, 3)),
            pltpu.SemaphoreType.DMA((QUARTERS,)),
        ],
        compiler_params=VMEM,
        name="corrected",
    )(*in_hbm(layer_input, output_grad, feedback, basis_prev))


def eliminate(factor):
    rank, columns = factor.shape
    both = jnp.concatenate([factor, factor], 0)
    gram = lax.dot_general(
        factor,
        both,
        (((1,), (1,)), ((), ())),
        preferred_element_type=jnp.float32,
        precision=lax.Precision.HIGHEST,
    )
    blocks = rank // 8
    lanes = columns // 128
    table = [
        [gram[8 * i : 8 * i + 8]]
        + [factor[8 * i : 8 * i + 8, 128 * j : 128 * j + 128] for j in range(lanes)]
        for i in range(blocks)
    ]
    sublane = lax.broadcasted_iota(jnp.int32, (8, 128), 0)
    spread = lambda row: jnp.broadcast_to(row, (8, 128))
    out = []
    for p in range(blocks):
        below = range(p, blocks)
        col = [
            {i: jnp.broadcast_to(table[i][0][:, 8 * p + j : 8 * p + j + 1], (8, 128)) for i in below}
            for j in range(8)
        ]
        pivots = jnp.ones((8, 128), jnp.float32)
        for j in range(8):
            pivot = spread(col[j][p][j : j + 1])
            pivots = jnp.where(sublane == j, pivot, pivots)
            if p == blocks - 1 and j == 7:
                break
            inverse = 1.0 / pivot
            mult = {i: col[j][i] * inverse for i in below}
            mult[p] = jnp.where(sublane > j, mult[p], 0.0)
            for k in range(j + 1, 8):
                entry = spread(col[j][p][k : k + 1])
                for i in below:
                    col[k][i] = col[k][i] - mult[i] * entry
            for t in range(lanes + 1):
                if t == 0 and p == blocks - 1:
                    continue
                row = spread(table[p][t][j : j + 1])
                for i in below:
                    table[i][t] = table[i][t] - mult[i] * row
        scale = lax.rsqrt(pivots)
        out.append([table[p][t] * scale for t in range(1, lanes + 1)])
    return out


def factor_kernel(me_ref, tiles_ref, corrected_hbm, left_ref, low_ref, *rest):
    term_refs, (corrected_ref, sem) = rest[:QUARTERS], rest[QUARTERS:]
    me = me_ref[0]
    fetch = pltpu.make_async_copy(corrected_hbm, corrected_ref, sem)
    fetch.start()
    rank, columns = left_ref.shape
    lanes = columns // 128
    factor = jnp.concatenate(
        [
            jnp.concatenate([tiles_ref[i * lanes + j] for j in range(lanes)], 1)
            for i in range(rank // 8)
        ],
        0,
    )
    blocks = eliminate(factor)
    for i, block in enumerate(blocks):
        for j, tile in enumerate(block):
            left_ref[8 * i : 8 * i + 8, 128 * j : 128 * j + 128] = tile
    low = left_ref[...].astype(jnp.bfloat16)
    low_ref[...] = low
    fetch.wait()
    for k in range(QUARTERS):
        quarter = lax.rem(me + k, QUARTERS)
        term_refs[k][...] = jnp.dot(low, corrected_ref[quarter], preferred_element_type=jnp.float32)


def factor_and_terms(me, tiles, corrected, rank):
    quarters, rows, width = corrected.shape
    whole = pl.BlockSpec(memory_space=pltpu.VMEM)
    return pl.pallas_call(
        factor_kernel,
        in_specs=[
            pl.BlockSpec(memory_space=pltpu.SMEM),
            whole,
            pl.BlockSpec(memory_space=pltpu.HBM),
        ],
        out_specs=[whole] * (2 + quarters),
        out_shape=[
            jax.ShapeDtypeStruct((rank, rows), jnp.float32),
            jax.ShapeDtypeStruct((rank, rows), jnp.bfloat16),
        ]
        + [jax.ShapeDtypeStruct((rank, width), jnp.float32)] * quarters,
        scratch_shapes=[pltpu.VMEM(corrected.shape, jnp.bfloat16), pltpu.SemaphoreType.DMA(())],
        compiler_params=VMEM,
        name="factor",
    )(me, tiles, *in_hbm(corrected))


def subtract(quarter, total_ref, low_t_ref, corrected_ref, next_hbm, feedback_hbm, next_ref, out_ref, sems):
    rows, width = out_ref.shape
    height = rows // STRIPS
    columns = pl.ds(pl.multiple_of(quarter * width, 128), width)
    basis_next = total_ref[...] * (1.0 / REPLICAS)
    next_ref[...] = basis_next
    stores = [pltpu.make_async_copy(next_ref, next_hbm.at[:, columns], sems.at[STRIPS])]
    stores[0].start()
    basis_round = basis_next.astype(jnp.bfloat16)
    for i in range(STRIPS):
        strip = pl.ds(i * height, height)
        approx = jnp.dot(low_t_ref[strip], basis_round, preferred_element_type=jnp.float32)
        out_ref[strip] = (corrected_ref[strip].astype(jnp.float32) - approx).astype(jnp.bfloat16)
        stores.append(
            pltpu.make_async_copy(out_ref.at[strip], feedback_hbm.at[strip, columns], sems.at[i])
        )
        stores[-1].start()
    return stores


def own_quarter_kernel(
    me_ref, total_ref, low_t_ref, corrected_hbm, next_hbm, feedback_hbm, *rest
):
    other_refs, (next_ref, out_ref, own_ref, sems, fetch_sems) = rest[: QUARTERS - 1], rest[QUARTERS - 1 :]
    me = me_ref[0]
    places = [own_ref] + list(other_refs)
    fetches = [
        pltpu.make_async_copy(
            corrected_hbm.at[lax.rem(me + (QUARTERS - k), QUARTERS)], places[k], fetch_sems.at[k]
        )
        for k in range(QUARTERS)
    ]
    for k in ARRIVING:
        fetches[k].start()
    fetches[0].wait()
    stores = subtract(me, total_ref, low_t_ref, own_ref, next_hbm, feedback_hbm, next_ref, out_ref, sems)
    for k in ARRIVING[1:]:
        fetches[k].wait()
    for store in stores:
        store.wait()


def other_quarter_kernel(
    me_ref, total_ref, low_t_ref, corrected_ref, next_in, feedback_in, next_hbm, feedback_hbm, next_ref, out_ref, sems, *, k
):
    quarter = lax.rem(me_ref[0] + (QUARTERS - k), QUARTERS)
    for store in subtract(
        quarter, total_ref, low_t_ref, corrected_ref, next_hbm, feedback_hbm, next_ref, out_ref, sems
    ):
        store.wait()


def finish(me, totals, low_t, corrected):
    quarters, rows, width = corrected.shape
    rank = low_t.shape[1]
    hbm = pl.BlockSpec(memory_space=pltpu.HBM)
    whole = pl.BlockSpec(memory_space=pltpu.VMEM)
    scalar = pl.BlockSpec(memory_space=pltpu.SMEM)
    outputs = [
        pltpu.HBM((rank, width * quarters), jnp.float32),
        pltpu.HBM((rows, width * quarters), jnp.bfloat16),
    ]
    scratch = [
        pltpu.VMEM((rank, width), jnp.float32),
        pltpu.VMEM((rows, width), jnp.bfloat16),
    ]
    *results, first, second, third = pl.pallas_call(
        own_quarter_kernel,
        in_specs=[scalar, whole, whole, hbm],
        out_specs=[hbm, hbm] + [whole] * (quarters - 1),
        out_shape=outputs + [pltpu.VMEM((rows, width), jnp.bfloat16)] * (quarters - 1),
        scratch_shapes=scratch
        + [
            pltpu.VMEM((rows, width), jnp.bfloat16),
            pltpu.SemaphoreType.DMA((STRIPS + 1,)),
            pltpu.SemaphoreType.DMA((quarters,)),
        ],
        compiler_params=VMEM,
        name="own_quarter",
    )(me, totals[0], low_t, *in_hbm(corrected))
    blocks = [None, first, second, third]
    for k in ARRIVING[1:]:
        results = pl.pallas_call(
            functools.partial(other_quarter_kernel, k=k),
            in_specs=[scalar, whole, whole, whole, hbm, hbm],
            out_specs=[hbm, hbm],
            out_shape=outputs,
            scratch_shapes=scratch + [pltpu.SemaphoreType.DMA((STRIPS + 1,))],
            input_output_aliases={4: 0, 5: 1},
            compiler_params=VMEM,
            name="quarter",
        )(me, totals[k], low_t, *in_vmem(blocks[k]), *in_hbm(*results))
    return results


def local(layer_input, output_grad, feedback, basis_prev):
    me = lax.axis_index("x").reshape(1)
    corrected, tiles = corrected_and_factor(layer_input, output_grad, feedback, basis_prev)
    tiles, me = lax.optimization_barrier((tiles, me))
    tiles = sum_all(tiles)
    factor_left, factor_low, *terms = factor_and_terms(me, tiles, corrected, basis_prev.shape[0])
    factor_low_t = factor_low.T

    arrived = [shift(terms[k], "x", k) for k in range(1, QUARTERS)]
    quarter = terms[0] + sum(arrived)
    piece = lax.all_to_all(quarter.reshape(SIZES["z"], 8, -1), "z", 0, 0, tiled=True)
    piece = jnp.sum(piece, 0)
    quarter = copies(piece, ("z",)).reshape(quarter.shape)
    totals = [quarter] + [shift(quarter, "x", k) for k in range(1, QUARTERS)]
    results = finish(me, totals, factor_low_t, corrected)
    return (factor_left,) + tuple(results)


def solution(mesh):
    fine = Mesh(mesh.devices.reshape(8, 4, 4, 2), ("z", "x", "y", "c"))
    dp, tensor = ("z", "x"), ("y", "c")
    in_specs = (P(dp, None), P(dp, tensor), P(dp, tensor), P(None, tensor))
    out_specs = (P(), P(None, tensor), P(dp, tensor))
    return jax.shard_map(local, mesh=fine, in_specs=in_specs, out_specs=out_specs, check_vma=False)
```

```python
import math

import jax
import jax.numpy as jnp
from jax import lax
from jax.experimental import pallas as pl
from jax.experimental.pallas import tpu as pltpu
from jax.sharding import Mesh
from jax.sharding import PartitionSpec as P

SIZES = dict(zh=4, zl=2, x=4, y=4, c=2)
PLANE = ("x", "y", "c")
LINE = ("zh", "zl")
NEAR = ("zl", "x")
REPLICAS = SIZES["zh"] * SIZES["zl"] * SIZES["x"]
QUARTERS = SIZES["x"]
HALVES = SIZES["zl"]
EARLY = 2
VMEM = pltpu.CompilerParams(vmem_limit_bytes=20 << 20)


def in_hbm(*arrays):
    return [pltpu.with_memory_space_constraint(a, pltpu.HBM) for a in arrays]


def in_vmem(*arrays):
    return [pltpu.with_memory_space_constraint(a, pltpu.VMEM) for a in arrays]


def shift(block, axis, step):
    n = SIZES[axis]
    return lax.ppermute(block, axis, [(i, (i + step) % n) for i in range(n)])


def copies(block, axes):
    n = math.prod(SIZES[a] for a in axes)
    sent = jnp.broadcast_to(block[None], (n,) + block.shape)
    return lax.all_to_all(sent, axes, 0, 0, tiled=True)


def sum_all(tiles):
    parts = lax.all_to_all(tiles, PLANE, 0, 0, tiled=True)
    parts = copies(jnp.sum(parts, 0), LINE)
    return copies(jnp.sum(parts, 0), PLANE)


def corrected_kernel(
    x_hbm, g_hbm, fb_hbm, basis_hbm, corrected_hbm, tiles_ref,
    x_ref, g_ref, fb_ref, basis_ref, out_ref, x_sem, in_sems, out_sems,
):
    width = g_ref.shape[2]
    fetch_x = pltpu.make_async_copy(x_hbm, x_ref, x_sem)
    fetch_x.start()
    fetches = []
    for q in range(QUARTERS):
        columns = pl.ds(q * width, width)
        pairs = ((g_hbm, g_ref), (fb_hbm, fb_ref), (basis_hbm, basis_ref))
        fetches.append(
            [
                pltpu.make_async_copy(whole.at[:, columns], part.at[q], in_sems.at[q, i])
                for i, (whole, part) in enumerate(pairs)
            ]
        )
        for fetch in fetches[q]:
            fetch.start()
    fetch_x.wait()
    xt = x_ref[...].T

    def factor_part(q):
        return lax.dot_general(
            basis_ref[q].astype(jnp.bfloat16),
            out_ref[q],
            (((1,), (1,)), ((), ())),
            preferred_element_type=jnp.float32,
        )

    parts = []
    stores = []
    for q in range(QUARTERS):
        for fetch in fetches[q]:
            fetch.wait()
        grad = jnp.dot(xt, g_ref[q], preferred_element_type=jnp.float32)
        if q:
            parts.append(factor_part(q - 1))
        grad = grad * (1.0 / math.sqrt(x_ref.shape[0])) + fb_ref[q].astype(jnp.float32)
        out_ref[q] = grad.astype(jnp.bfloat16)
        stores.append(pltpu.make_async_copy(out_ref.at[q], corrected_hbm.at[q], out_sems.at[q]))
        stores[q].start()
    parts.append(factor_part(QUARTERS - 1))
    total = sum(parts[1:], parts[0])
    rows, columns = total.shape
    for i in range(rows // 8):
        for j in range(columns // 128):
            tiles_ref[i * (columns // 128) + j] = total[8 * i : 8 * i + 8, 128 * j : 128 * j + 128]
    for store in stores:
        store.wait()


def corrected_and_factor(layer_input, output_grad, feedback, basis_prev):
    tokens, rows = layer_input.shape
    columns, rank = output_grad.shape[1], basis_prev.shape[0]
    width = columns // QUARTERS
    return pl.pallas_call(
        corrected_kernel,
        in_specs=[pl.BlockSpec(memory_space=pltpu.HBM)] * 4,
        out_specs=[pl.BlockSpec(memory_space=pltpu.HBM), pl.BlockSpec(memory_space=pltpu.VMEM)],
        out_shape=[
            pltpu.HBM((QUARTERS, rows, width), jnp.bfloat16),
            jax.ShapeDtypeStruct((rank * rows // 1024, 8, 128), jnp.float32),
        ],
        scratch_shapes=[
            pltpu.VMEM((tokens, rows), jnp.bfloat16),
            pltpu.VMEM((QUARTERS, tokens, width), jnp.bfloat16),
            pltpu.VMEM((QUARTERS, rows, width), jnp.bfloat16),
            pltpu.VMEM((QUARTERS, rank, width), jnp.float32),
            pltpu.VMEM((QUARTERS, rows, width), jnp.bfloat16),
            pltpu.SemaphoreType.DMA(()),
            pltpu.SemaphoreType.DMA((QUARTERS, 3)),
            pltpu.SemaphoreType.DMA((QUARTERS,)),
        ],
        compiler_params=VMEM,
        name="corrected",
    )(*in_hbm(layer_input, output_grad, feedback, basis_prev))


def eliminate(factor):
    rank, columns = factor.shape
    both = jnp.concatenate([factor, factor], 0)
    gram = lax.dot_general(
        factor,
        both,
        (((1,), (1,)), ((), ())),
        preferred_element_type=jnp.float32,
        precision=lax.Precision.HIGHEST,
    )
    blocks = rank // 8
    lanes = columns // 128
    table = [
        [gram[8 * i : 8 * i + 8]]
        + [factor[8 * i : 8 * i + 8, 128 * j : 128 * j + 128] for j in range(lanes)]
        for i in range(blocks)
    ]
    sublane = lax.broadcasted_iota(jnp.int32, (8, 128), 0)
    spread = lambda row: jnp.broadcast_to(row, (8, 128))
    out = []
    for p in range(blocks):
        below = range(p, blocks)
        col = [
            {i: jnp.broadcast_to(table[i][0][:, 8 * p + j : 8 * p + j + 1], (8, 128)) for i in below}
            for j in range(8)
        ]
        pivots = jnp.ones((8, 128), jnp.float32)
        for j in range(8):
            pivot = spread(col[j][p][j : j + 1])
            pivots = jnp.where(sublane == j, pivot, pivots)
            if p == blocks - 1 and j == 7:
                break
            inverse = 1.0 / pivot
            mult = {i: col[j][i] * inverse for i in below}
            mult[p] = jnp.where(sublane > j, mult[p], 0.0)
            for k in range(j + 1, 8):
                entry = spread(col[j][p][k : k + 1])
                for i in below:
                    col[k][i] = col[k][i] - mult[i] * entry
            for t in range(lanes + 1):
                if t == 0 and p == blocks - 1:
                    continue
                row = spread(table[p][t][j : j + 1])
                for i in below:
                    table[i][t] = table[i][t] - mult[i] * row
        scale = lax.rsqrt(pivots)
        out.append([table[p][t] * scale for t in range(1, lanes + 1)])
    return out


def factor_kernel(tiles_ref, corrected_hbm, left_ref, low_ref, terms_ref, corrected_ref, sem):
    fetch = pltpu.make_async_copy(corrected_hbm, corrected_ref, sem)
    fetch.start()
    rank, columns = left_ref.shape
    lanes = columns // 128
    factor = jnp.concatenate(
        [
            jnp.concatenate([tiles_ref[i * lanes + j] for j in range(lanes)], 1)
            for i in range(rank // 8)
        ],
        0,
    )
    blocks = eliminate(factor)
    for i, block in enumerate(blocks):
        for j, tile in enumerate(block):
            left_ref[8 * i : 8 * i + 8, 128 * j : 128 * j + 128] = tile
    low = left_ref[...].astype(jnp.bfloat16)
    low_ref[...] = low
    fetch.wait()
    for q in range(QUARTERS):
        term = jnp.dot(low, corrected_ref[q], preferred_element_type=jnp.float32)
        for h in range(HALVES):
            terms_ref[h * QUARTERS + q] = term[h * (rank // HALVES) : (h + 1) * (rank // HALVES)]


def factor_and_terms(tiles, corrected, rank):
    quarters, rows, width = corrected.shape
    whole = pl.BlockSpec(memory_space=pltpu.VMEM)
    return pl.pallas_call(
        factor_kernel,
        in_specs=[whole, pl.BlockSpec(memory_space=pltpu.HBM)],
        out_specs=[whole] * 3,
        out_shape=[
            jax.ShapeDtypeStruct((rank, rows), jnp.float32),
            jax.ShapeDtypeStruct((rank, rows), jnp.bfloat16),
            jax.ShapeDtypeStruct((HALVES * quarters, rank // HALVES, width), jnp.float32),
        ],
        scratch_shapes=[pltpu.VMEM(corrected.shape, jnp.bfloat16), pltpu.SemaphoreType.DMA(())],
        compiler_params=VMEM,
        name="factor",
    )(tiles, *in_hbm(corrected))


def fetch_kernel(after_ref, low_ref, corrected_hbm, low_t_ref, fetched_ref, sem):
    fetch = pltpu.make_async_copy(corrected_hbm.at[pl.ds(0, EARLY)], fetched_ref, sem)
    fetch.start()
    low_t_ref[...] = low_ref[...].astype(jnp.float32).T.astype(jnp.bfloat16)
    fetch.wait()


def fetch_after(before, low, corrected):
    rank, rows = low.shape
    whole = pl.BlockSpec(memory_space=pltpu.VMEM)
    return pl.pallas_call(
        fetch_kernel,
        in_specs=[pl.BlockSpec(memory_space=pl.ANY), whole, pl.BlockSpec(memory_space=pltpu.HBM)],
        out_specs=[whole, whole],
        out_shape=[
            pltpu.VMEM((rows, rank), low.dtype),
            pltpu.VMEM((EARLY,) + corrected.shape[1:], corrected.dtype),
        ],
        scratch_shapes=[pltpu.SemaphoreType.DMA(())],
        compiler_params=VMEM,
        name="fetch",
    )(before, low, *in_hbm(corrected))


def feedback_kernel(
    total_ref, low_t_ref, early_ref, corrected_hbm, next_hbm, feedback_hbm, next_ref, out_ref, late_ref, sems, late_sems
):
    quarters, rows, width = out_ref.shape
    fetches = [
        pltpu.make_async_copy(corrected_hbm.at[q], late_ref.at[q - EARLY], late_sems.at[q - EARLY])
        for q in range(EARLY, quarters)
    ]
    for fetch in fetches:
        fetch.start()
    stores = []
    for q in range(quarters):
        columns = pl.ds(q * width, width)
        basis_next = jnp.concatenate([total_ref[h * quarters + q] for h in range(HALVES)], 0) * (1.0 / REPLICAS)
        next_ref[q] = basis_next
        stores.append(pltpu.make_async_copy(next_ref.at[q], next_hbm.at[:, columns], sems.at[0, q]))
        stores[-1].start()
        approx = jnp.dot(
            low_t_ref[...], basis_next.astype(jnp.bfloat16), preferred_element_type=jnp.float32
        )
        if q >= EARLY:
            fetches[q - EARLY].wait()
        corrected = early_ref[q] if q < EARLY else late_ref[q - EARLY]
        out_ref[q] = (corrected.astype(jnp.float32) - approx).astype(jnp.bfloat16)
        stores.append(pltpu.make_async_copy(out_ref.at[q], feedback_hbm.at[:, columns], sems.at[1, q]))
        stores[-1].start()
    for store in stores:
        store.wait()


def finish(total, low_t, early, corrected):
    quarters, rows, width = corrected.shape
    rank = low_t.shape[1]
    hbm = pl.BlockSpec(memory_space=pltpu.HBM)
    whole = pl.BlockSpec(memory_space=pltpu.VMEM)
    return pl.pallas_call(
        feedback_kernel,
        in_specs=[whole, whole, whole, hbm],
        out_specs=[hbm, hbm],
        out_shape=[
            pltpu.HBM((rank, width * quarters), jnp.float32),
            pltpu.HBM((rows, width * quarters), jnp.bfloat16),
        ],
        scratch_shapes=[
            pltpu.VMEM((quarters, rank, width), jnp.float32),
            pltpu.VMEM((quarters, rows, width), jnp.bfloat16),
            pltpu.VMEM((quarters - EARLY, rows, width), jnp.bfloat16),
            pltpu.SemaphoreType.DMA((2, quarters)),
            pltpu.SemaphoreType.DMA((quarters - EARLY,)),
        ],
        compiler_params=VMEM,
        name="feedback",
    )(total, *in_vmem(low_t, early), *in_hbm(corrected))


def local(layer_input, output_grad, feedback, basis_prev):
    corrected, tiles = corrected_and_factor(layer_input, output_grad, feedback, basis_prev)
    tiles = sum_all(tiles)
    factor_left, factor_low, terms = factor_and_terms(tiles, corrected, basis_prev.shape[0])

    block = jnp.sum(lax.all_to_all(terms, NEAR, 0, 0, tiled=True), 0)
    one, two, three = (shift(block, "zh", k) for k in (1, 2, 3))
    low_t, early = fetch_after(block, factor_low, corrected)
    block = (block + two) + (one + three)
    block, low_t, early = lax.optimization_barrier((block, low_t, early))
    basis_next, feedback_next = finish(copies(block, NEAR), low_t, early, corrected)
    return factor_left, basis_next, feedback_next


def solution(mesh):
    fine = Mesh(mesh.devices.reshape(4, 2, 4, 4, 2), ("zh", "zl", "x", "y", "c"))
    dp, tensor = ("zh", "zl", "x"), ("y", "c")
    in_specs = (P(dp, None), P(dp, tensor), P(dp, tensor), P(None, tensor))
    out_specs = (P(), P(None, tensor), P(dp, tensor))
    return jax.shard_map(local, mesh=fine, in_specs=in_specs, out_specs=out_specs, check_vma=False)
```

```python
import math

import jax
import jax.numpy as jnp
from jax import lax
from jax.experimental import pallas as pl
from jax.experimental.pallas import tpu as pltpu
from jax.sharding import Mesh
from jax.sharding import PartitionSpec as P

SIZES = dict(zh=4, zl=2, x=4, y=4, c=2)
PLANE = ("x", "y", "c")
LINE = ("zh", "zl")
NEAR = ("zl", "x")
REPLICAS = SIZES["zh"] * SIZES["zl"] * SIZES["x"]
QUARTERS = SIZES["x"]
HALVES = SIZES["zl"]
AHEAD = 2
EARLY = 2
VMEM = pltpu.CompilerParams(vmem_limit_bytes=20 << 20)


def in_hbm(*arrays):
    return [pltpu.with_memory_space_constraint(a, pltpu.HBM) for a in arrays]


def in_vmem(*arrays):
    return [pltpu.with_memory_space_constraint(a, pltpu.VMEM) for a in arrays]


def shift(block, axis, step):
    n = SIZES[axis]
    return lax.ppermute(block, axis, [(i, (i + step) % n) for i in range(n)])


def copies(block, axes):
    n = math.prod(SIZES[a] for a in axes)
    sent = jnp.broadcast_to(block[None], (n,) + block.shape)
    return lax.all_to_all(sent, axes, 0, 0, tiled=True)


def sum_all(tiles):
    parts = lax.all_to_all(tiles, PLANE, 0, 0, tiled=True)
    parts = copies(jnp.sum(parts, 0), LINE)
    return copies(jnp.sum(parts, 0), PLANE)


def corrected_kernel(
    x_hbm, g_hbm, fb_hbm, basis_hbm, early_ref, late_hbm, tiles_ref,
    x_ref, g_ref, fb_ref, basis_ref, late_ref, x_sem, in_sems, out_sems,
):
    width = g_ref.shape[2]
    fetch_x = pltpu.make_async_copy(x_hbm, x_ref, x_sem)
    fetch_x.start()
    fetches = []
    for q in range(QUARTERS):
        columns = pl.ds(q * width, width)
        pairs = ((g_hbm, g_ref), (fb_hbm, fb_ref), (basis_hbm, basis_ref))
        fetches.append(
            [
                pltpu.make_async_copy(whole.at[:, columns], part.at[q], in_sems.at[q, i])
                for i, (whole, part) in enumerate(pairs)
            ]
        )
    for q in range(AHEAD):
        for fetch in fetches[q]:
            fetch.start()
    fetch_x.wait()
    xt = x_ref[...].T
    corrected = lambda q: early_ref.at[q] if q < EARLY else late_ref.at[q - EARLY]

    def factor_part(q):
        return lax.dot_general(
            basis_ref[q].astype(jnp.bfloat16),
            corrected(q)[...],
            (((1,), (1,)), ((), ())),
            preferred_element_type=jnp.float32,
        )

    parts = []
    stores = []
    for q in range(QUARTERS):
        for fetch in fetches[q]:
            fetch.wait()
        if q + AHEAD < QUARTERS:
            for fetch in fetches[q + AHEAD]:
                fetch.start()
        grad = jnp.dot(xt, g_ref[q], preferred_element_type=jnp.float32)
        if q:
            parts.append(factor_part(q - 1))
        grad = grad * (1.0 / math.sqrt(x_ref.shape[0])) + fb_ref[q].astype(jnp.float32)
        corrected(q)[...] = grad.astype(jnp.bfloat16)
        if q >= EARLY:
            late = q - EARLY
            stores.append(pltpu.make_async_copy(late_ref.at[late], late_hbm.at[late], out_sems.at[late]))
            stores[-1].start()
    parts.append(factor_part(QUARTERS - 1))
    total = sum(parts[1:], parts[0])
    rows, columns = total.shape
    for i in range(rows // 8):
        for j in range(columns // 128):
            tiles_ref[i * (columns // 128) + j] = total[8 * i : 8 * i + 8, 128 * j : 128 * j + 128]
    for store in stores:
        store.wait()


def corrected_and_factor(layer_input, output_grad, feedback, basis_prev):
    tokens, rows = layer_input.shape
    columns, rank = output_grad.shape[1], basis_prev.shape[0]
    width = columns // QUARTERS
    return pl.pallas_call(
        corrected_kernel,
        in_specs=[pl.BlockSpec(memory_space=pltpu.HBM)] * 4,
        out_specs=[pl.BlockSpec(memory_space=space) for space in (pltpu.VMEM, pltpu.HBM, pltpu.VMEM)],
        out_shape=[
            pltpu.VMEM((EARLY, rows, width), jnp.bfloat16),
            pltpu.HBM((QUARTERS - EARLY, rows, width), jnp.bfloat16),
            jax.ShapeDtypeStruct((rank * rows // 1024, 8, 128), jnp.float32),
        ],
        scratch_shapes=[
            pltpu.VMEM((tokens, rows), jnp.bfloat16),
            pltpu.VMEM((QUARTERS, tokens, width), jnp.bfloat16),
            pltpu.VMEM((QUARTERS, rows, width), jnp.bfloat16),
            pltpu.VMEM((QUARTERS, rank, width), jnp.float32),
            pltpu.VMEM((QUARTERS - EARLY, rows, width), jnp.bfloat16),
            pltpu.SemaphoreType.DMA(()),
            pltpu.SemaphoreType.DMA((QUARTERS, 3)),
            pltpu.SemaphoreType.DMA((QUARTERS - EARLY,)),
        ],
        compiler_params=VMEM,
        name="corrected",
    )(*in_hbm(layer_input, output_grad, feedback, basis_prev))


def eliminate(factor):
    rank, columns = factor.shape
    both = jnp.concatenate([factor, factor], 0)
    gram = lax.dot_general(
        factor,
        both,
        (((1,), (1,)), ((), ())),
        preferred_element_type=jnp.float32,
        precision=lax.Precision.HIGHEST,
    )
    blocks = rank // 8
    lanes = columns // 128
    table = [
        [gram[8 * i : 8 * i + 8]]
        + [factor[8 * i : 8 * i + 8, 128 * j : 128 * j + 128] for j in range(lanes)]
        for i in range(blocks)
    ]
    sublane = lax.broadcasted_iota(jnp.int32, (8, 128), 0)
    spread = lambda row: jnp.broadcast_to(row, (8, 128))
    out = []
    for p in range(blocks):
        below = range(p, blocks)
        col = [
            {i: jnp.broadcast_to(table[i][0][:, 8 * p + j : 8 * p + j + 1], (8, 128)) for i in below}
            for j in range(8)
        ]
        pivots = jnp.ones((8, 128), jnp.float32)
        for j in range(8):
            pivot = spread(col[j][p][j : j + 1])
            pivots = jnp.where(sublane == j, pivot, pivots)
            if p == blocks - 1 and j == 7:
                break
            inverse = 1.0 / pivot
            mult = {i: col[j][i] * inverse for i in below}
            mult[p] = jnp.where(sublane > j, mult[p], 0.0)
            for k in range(j + 1, 8):
                entry = spread(col[j][p][k : k + 1])
                for i in below:
                    col[k][i] = col[k][i] - mult[i] * entry
            for t in range(lanes + 1):
                if t == 0 and p == blocks - 1:
                    continue
                row = spread(table[p][t][j : j + 1])
                for i in below:
                    table[i][t] = table[i][t] - mult[i] * row
        scale = lax.rsqrt(pivots)
        out.append([table[p][t] * scale for t in range(1, lanes + 1)])
    return out


def factor_kernel(tiles_ref, early_ref, late_hbm, left_ref, low_ref, terms_ref, late_ref, sem):
    fetch = pltpu.make_async_copy(late_hbm, late_ref, sem)
    fetch.start()
    rank, columns = left_ref.shape
    lanes = columns // 128
    factor = jnp.concatenate(
        [
            jnp.concatenate([tiles_ref[i * lanes + j] for j in range(lanes)], 1)
            for i in range(rank // 8)
        ],
        0,
    )
    blocks = eliminate(factor)
    for i, block in enumerate(blocks):
        for j, tile in enumerate(block):
            left_ref[8 * i : 8 * i + 8, 128 * j : 128 * j + 128] = tile
    low = left_ref[...].astype(jnp.bfloat16)
    low_ref[...] = low
    for q in range(QUARTERS):
        if q == EARLY:
            fetch.wait()
        corrected = early_ref[q] if q < EARLY else late_ref[q - EARLY]
        term = jnp.dot(low, corrected, preferred_element_type=jnp.float32)
        for h in range(HALVES):
            terms_ref[h * QUARTERS + q] = term[h * (rank // HALVES) : (h + 1) * (rank // HALVES)]


def factor_and_terms(tiles, early, late, rank):
    _, rows, width = late.shape
    whole = pl.BlockSpec(memory_space=pltpu.VMEM)
    return pl.pallas_call(
        factor_kernel,
        in_specs=[whole, whole, pl.BlockSpec(memory_space=pltpu.HBM)],
        out_specs=[whole] * 3,
        out_shape=[
            jax.ShapeDtypeStruct((rank, rows), jnp.float32),
            jax.ShapeDtypeStruct((rank, rows), jnp.bfloat16),
            jax.ShapeDtypeStruct((HALVES * QUARTERS, rank // HALVES, width), jnp.float32),
        ],
        scratch_shapes=[pltpu.VMEM(late.shape, jnp.bfloat16), pltpu.SemaphoreType.DMA(())],
        compiler_params=VMEM,
        name="factor",
    )(tiles, *in_vmem(early), *in_hbm(late))


def transpose_kernel(after_ref, low_ref, low_t_ref):
    low_t_ref[...] = low_ref[...].astype(jnp.float32).T.astype(jnp.bfloat16)


def transposed_after(before, low):
    return pl.pallas_call(
        transpose_kernel,
        in_specs=[pl.BlockSpec(memory_space=pl.ANY), pl.BlockSpec(memory_space=pltpu.VMEM)],
        out_specs=pl.BlockSpec(memory_space=pltpu.VMEM),
        out_shape=pltpu.VMEM(low.shape[::-1], low.dtype),
        compiler_params=VMEM,
        name="transpose",
    )(before, low)


def feedback_kernel(
    total_ref, low_t_ref, early_ref, late_hbm, next_hbm, feedback_hbm, next_ref, out_ref, late_ref, sems, late_sems
):
    quarters, rows, width = out_ref.shape
    fetches = [
        pltpu.make_async_copy(late_hbm.at[i], late_ref.at[i], late_sems.at[i])
        for i in range(late_ref.shape[0])
    ]
    for fetch in fetches:
        fetch.start()
    stores = []
    for q in range(quarters):
        columns = pl.ds(q * width, width)
        basis_next = jnp.concatenate([total_ref[h * quarters + q] for h in range(HALVES)], 0) * (1.0 / REPLICAS)
        next_ref[q] = basis_next
        stores.append(pltpu.make_async_copy(next_ref.at[q], next_hbm.at[:, columns], sems.at[0, q]))
        stores[-1].start()
        approx = jnp.dot(
            low_t_ref[...], basis_next.astype(jnp.bfloat16), preferred_element_type=jnp.float32
        )
        if q >= EARLY:
            fetches[q - EARLY].wait()
        corrected = early_ref[q] if q < EARLY else late_ref[q - EARLY]
        out_ref[q] = (corrected.astype(jnp.float32) - approx).astype(jnp.bfloat16)
        stores.append(pltpu.make_async_copy(out_ref.at[q], feedback_hbm.at[:, columns], sems.at[1, q]))
        stores[-1].start()
    for store in stores:
        store.wait()


def finish(total, low_t, early, late):
    _, rows, width = late.shape
    quarters = QUARTERS
    rank = low_t.shape[1]
    hbm = pl.BlockSpec(memory_space=pltpu.HBM)
    whole = pl.BlockSpec(memory_space=pltpu.VMEM)
    return pl.pallas_call(
        feedback_kernel,
        in_specs=[whole, whole, whole, hbm],
        out_specs=[hbm, hbm],
        out_shape=[
            pltpu.HBM((rank, width * quarters), jnp.float32),
            pltpu.HBM((rows, width * quarters), jnp.bfloat16),
        ],
        scratch_shapes=[
            pltpu.VMEM((quarters, rank, width), jnp.float32),
            pltpu.VMEM((quarters, rows, width), jnp.bfloat16),
            pltpu.VMEM((quarters - EARLY, rows, width), jnp.bfloat16),
            pltpu.SemaphoreType.DMA((2, quarters)),
            pltpu.SemaphoreType.DMA((quarters - EARLY,)),
        ],
        compiler_params=VMEM,
        name="feedback",
    )(total, *in_vmem(low_t, early), *in_hbm(late))


def local(layer_input, output_grad, feedback, basis_prev):
    early, late, tiles = corrected_and_factor(layer_input, output_grad, feedback, basis_prev)
    tiles = sum_all(tiles)
    factor_left, factor_low, terms = factor_and_terms(tiles, early, late, basis_prev.shape[0])

    block = jnp.sum(lax.all_to_all(terms, NEAR, 0, 0, tiled=True), 0)
    one, two, three = (shift(block, "zh", k) for k in (1, 2, 3))
    low_t = transposed_after(block, factor_low)
    block = (block + two) + (one + three)
    block, low_t = lax.optimization_barrier((block, low_t))
    basis_next, feedback_next = finish(copies(block, NEAR), low_t, early, late)
    return factor_left, basis_next, feedback_next


def solution(mesh):
    fine = Mesh(mesh.devices.reshape(4, 2, 4, 4, 2), ("zh", "zl", "x", "y", "c"))
    dp, tensor = ("zh", "zl", "x"), ("y", "c")
    in_specs = (P(dp, None), P(dp, tensor), P(dp, tensor), P(None, tensor))
    out_specs = (P(), P(None, tensor), P(dp, tensor))
    return jax.shard_map(local, mesh=fine, in_specs=in_specs, out_specs=out_specs, check_vma=False)
```

```python
import math

import jax
import jax.numpy as jnp
from jax import lax
from jax.experimental import pallas as pl
from jax.experimental.pallas import tpu as pltpu
from jax.sharding import Mesh
from jax.sharding import PartitionSpec as P

SIZES = dict(zh=4, zl=2, x=4, y=4, c=2)
FIRST = ("zl", "x", "c")
REST = ("zh", "y")
NEAR = ("zl", "x")
REPLICAS = SIZES["zh"] * SIZES["zl"] * SIZES["x"]
QUARTERS = SIZES["x"]
HALVES = SIZES["zl"]
SPANS = 2
EARLY = 2
VMEM = pltpu.CompilerParams(vmem_limit_bytes=20 << 20)


def in_hbm(*arrays):
    return [pltpu.with_memory_space_constraint(a, pltpu.HBM) for a in arrays]


def in_vmem(*arrays):
    return [pltpu.with_memory_space_constraint(a, pltpu.VMEM) for a in arrays]


def shift(block, axis, step):
    n = SIZES[axis]
    return lax.ppermute(block, axis, [(i, (i + step) % n) for i in range(n)])


def copies(block, axes):
    n = math.prod(SIZES[a] for a in axes)
    sent = jnp.broadcast_to(block[None], (n,) + block.shape)
    return lax.all_to_all(sent, axes, 0, 0, tiled=True)


def sum_all(tiles):
    members = math.prod(SIZES[a] for a in FIRST)
    parts = lax.all_to_all(tiles, FIRST, 0, 0, tiled=True)
    piece = jnp.sum(parts.reshape((members, -1) + tiles.shape[1:]), 0)
    piece = jnp.sum(copies(piece, REST), 0)
    return copies(piece, FIRST).reshape(tiles.shape)


def corrected_kernel(
    x_hbm, g_hbm, fb_hbm, basis_hbm, early_ref, late_hbm, tiles_ref,
    x_ref, g_ref, fb_ref, basis_ref, late_ref, x_sem, in_sems, out_sems,
):
    span = g_ref.shape[2]
    width = early_ref.shape[2]
    fetch_x = pltpu.make_async_copy(x_hbm, x_ref, x_sem)
    fetch_x.start()
    fetches = []
    for n in range(SPANS):
        columns = pl.ds(n * span, span)
        pairs = ((g_hbm, g_ref), (fb_hbm, fb_ref), (basis_hbm, basis_ref))
        fetches.append(
            [
                pltpu.make_async_copy(whole.at[:, columns], part.at[n], in_sems.at[n, i])
                for i, (whole, part) in enumerate(pairs)
            ]
        )
        for fetch in fetches[n]:
            fetch.start()
    fetch_x.wait()
    xt = x_ref[...].T
    parts = []
    stores = []
    for n in range(SPANS):
        for fetch in fetches[n]:
            fetch.wait()
        grad = jnp.dot(xt, g_ref[n], preferred_element_type=jnp.float32)
        grad = grad * (1.0 / math.sqrt(x_ref.shape[0])) + fb_ref[n].astype(jnp.float32)
        corrected = grad.astype(jnp.bfloat16)
        for i in range(span // width):
            q = n * (span // width) + i
            piece = corrected[:, i * width : (i + 1) * width]
            if q < EARLY:
                early_ref[q] = piece
            else:
                late = q - EARLY
                late_ref[late] = piece
                stores.append(pltpu.make_async_copy(late_ref.at[late], late_hbm.at[late], out_sems.at[late]))
                stores[-1].start()
        parts.append(
            lax.dot_general(
                basis_ref[n].astype(jnp.bfloat16),
                corrected,
                (((1,), (1,)), ((), ())),
                preferred_element_type=jnp.float32,
            )
        )
    total = sum(parts[1:], parts[0])
    rows, columns = total.shape
    for i in range(rows // 8):
        for j in range(columns // 128):
            tiles_ref[i * (columns // 128) + j] = total[8 * i : 8 * i + 8, 128 * j : 128 * j + 128]
    for store in stores:
        store.wait()


def corrected_and_factor(layer_input, output_grad, feedback, basis_prev):
    tokens, rows = layer_input.shape
    columns, rank = output_grad.shape[1], basis_prev.shape[0]
    width = columns // QUARTERS
    return pl.pallas_call(
        corrected_kernel,
        in_specs=[pl.BlockSpec(memory_space=pltpu.HBM)] * 4,
        out_specs=[pl.BlockSpec(memory_space=space) for space in (pltpu.VMEM, pltpu.HBM, pltpu.VMEM)],
        out_shape=[
            pltpu.VMEM((EARLY, rows, width), jnp.bfloat16),
            pltpu.HBM((QUARTERS - EARLY, rows, width), jnp.bfloat16),
            jax.ShapeDtypeStruct((rank * rows // 1024, 8, 128), jnp.float32),
        ],
        scratch_shapes=[
            pltpu.VMEM((tokens, rows), jnp.bfloat16),
            pltpu.VMEM((SPANS, tokens, columns // SPANS), jnp.bfloat16),
            pltpu.VMEM((SPANS, rows, columns // SPANS), jnp.bfloat16),
            pltpu.VMEM((SPANS, rank, columns // SPANS), jnp.float32),
            pltpu.VMEM((QUARTERS - EARLY, rows, width), jnp.bfloat16),
            pltpu.SemaphoreType.DMA(()),
            pltpu.SemaphoreType.DMA((SPANS, 3)),
            pltpu.SemaphoreType.DMA((QUARTERS - EARLY,)),
        ],
        compiler_params=VMEM,
        name="corrected",
    )(*in_hbm(layer_input, output_grad, feedback, basis_prev))


def eliminate(factor):
    rank, columns = factor.shape
    both = jnp.concatenate([factor, factor], 0)
    gram = lax.dot_general(
        factor,
        both,
        (((1,), (1,)), ((), ())),
        preferred_element_type=jnp.float32,
        precision=lax.Precision.HIGHEST,
    )
    blocks = rank // 8
    lanes = columns // 128
    table = [
        [gram[8 * i : 8 * i + 8]]
        + [factor[8 * i : 8 * i + 8, 128 * j : 128 * j + 128] for j in range(lanes)]
        for i in range(blocks)
    ]
    sublane = lax.broadcasted_iota(jnp.int32, (8, 128), 0)
    spread = lambda row: jnp.broadcast_to(row, (8, 128))
    out = []
    for p in range(blocks):
        below = range(p, blocks)
        col = [
            {i: jnp.broadcast_to(table[i][0][:, 8 * p + j : 8 * p + j + 1], (8, 128)) for i in below}
            for j in range(8)
        ]
        pivots = jnp.ones((8, 128), jnp.float32)
        for j in range(8):
            pivot = spread(col[j][p][j : j + 1])
            pivots = jnp.where(sublane == j, pivot, pivots)
            if p == blocks - 1 and j == 7:
                break
            inverse = 1.0 / pivot
            mult = {i: col[j][i] * inverse for i in below}
            mult[p] = jnp.where(sublane > j, mult[p], 0.0)
            for k in range(j + 1, 8):
                entry = spread(col[j][p][k : k + 1])
                for i in below:
                    col[k][i] = col[k][i] - mult[i] * entry
            for t in range(lanes + 1):
                if t == 0 and p == blocks - 1:
                    continue
                row = spread(table[p][t][j : j + 1])
                for i in below:
                    table[i][t] = table[i][t] - mult[i] * row
        scale = lax.rsqrt(pivots)
        out.append([table[p][t] * scale for t in range(1, lanes + 1)])
    return out


def factor_kernel(tiles_ref, early_ref, late_hbm, left_ref, low_ref, terms_ref, late_ref, sem):
    fetch = pltpu.make_async_copy(late_hbm, late_ref, sem)
    fetch.start()
    rank, columns = left_ref.shape
    lanes = columns // 128
    factor = jnp.concatenate(
        [
            jnp.concatenate([tiles_ref[i * lanes + j] for j in range(lanes)], 1)
            for i in range(rank // 8)
        ],
        0,
    )
    blocks = eliminate(factor)
    for i, block in enumerate(blocks):
        for j, tile in enumerate(block):
            left_ref[8 * i : 8 * i + 8, 128 * j : 128 * j + 128] = tile
    low = left_ref[...].astype(jnp.bfloat16)
    low_ref[...] = low
    for q in range(QUARTERS):
        if q == EARLY:
            fetch.wait()
        corrected = early_ref[q] if q < EARLY else late_ref[q - EARLY]
        term = jnp.dot(low, corrected, preferred_element_type=jnp.float32)
        for h in range(HALVES):
            terms_ref[h * QUARTERS + q] = term[h * (rank // HALVES) : (h + 1) * (rank // HALVES)]


def factor_and_terms(tiles, early, late, rank):
    _, rows, width = late.shape
    whole = pl.BlockSpec(memory_space=pltpu.VMEM)
    return pl.pallas_call(
        factor_kernel,
        in_specs=[whole, whole, pl.BlockSpec(memory_space=pltpu.HBM)],
        out_specs=[whole] * 3,
        out_shape=[
            jax.ShapeDtypeStruct((rank, rows), jnp.float32),
            jax.ShapeDtypeStruct((rank, rows), jnp.bfloat16),
            jax.ShapeDtypeStruct((HALVES * QUARTERS, rank // HALVES, width), jnp.float32),
        ],
        scratch_shapes=[pltpu.VMEM(late.shape, jnp.bfloat16), pltpu.SemaphoreType.DMA(())],
        compiler_params=VMEM,
        name="factor",
    )(tiles, *in_vmem(early), *in_hbm(late))


def transpose_kernel(after_ref, low_ref, low_t_ref):
    low_t_ref[...] = low_ref[...].astype(jnp.float32).T.astype(jnp.bfloat16)


def transposed_after(before, low):
    return pl.pallas_call(
        transpose_kernel,
        in_specs=[pl.BlockSpec(memory_space=pl.ANY), pl.BlockSpec(memory_space=pltpu.VMEM)],
        out_specs=pl.BlockSpec(memory_space=pltpu.VMEM),
        out_shape=pltpu.VMEM(low.shape[::-1], low.dtype),
        compiler_params=VMEM,
        name="transpose",
    )(before, low)


def feedback_kernel(
    total_ref, low_t_ref, early_ref, late_hbm, next_hbm, feedback_hbm, next_ref, out_ref, late_ref, sems, late_sems
):
    quarters, rows, width = out_ref.shape
    fetches = [
        pltpu.make_async_copy(late_hbm.at[i], late_ref.at[i], late_sems.at[i])
        for i in range(late_ref.shape[0])
    ]
    for fetch in fetches:
        fetch.start()
    stores = []
    for q in range(quarters):
        columns = pl.ds(q * width, width)
        basis_next = jnp.concatenate([total_ref[h * quarters + q] for h in range(HALVES)], 0) * (1.0 / REPLICAS)
        next_ref[q] = basis_next
        stores.append(pltpu.make_async_copy(next_ref.at[q], next_hbm.at[:, columns], sems.at[0, q]))
        stores[-1].start()
        approx = jnp.dot(
            low_t_ref[...], basis_next.astype(jnp.bfloat16), preferred_element_type=jnp.float32
        )
        if q >= EARLY:
            fetches[q - EARLY].wait()
        corrected = early_ref[q] if q < EARLY else late_ref[q - EARLY]
        out_ref[q] = (corrected.astype(jnp.float32) - approx).astype(jnp.bfloat16)
        stores.append(pltpu.make_async_copy(out_ref.at[q], feedback_hbm.at[:, columns], sems.at[1, q]))
        stores[-1].start()
    for store in stores:
        store.wait()


def finish(total, low_t, early, late):
    _, rows, width = late.shape
    quarters = QUARTERS
    rank = low_t.shape[1]
    hbm = pl.BlockSpec(memory_space=pltpu.HBM)
    whole = pl.BlockSpec(memory_space=pltpu.VMEM)
    return pl.pallas_call(
        feedback_kernel,
        in_specs=[whole, whole, whole, hbm],
        out_specs=[hbm, hbm],
        out_shape=[
            pltpu.HBM((rank, width * quarters), jnp.float32),
            pltpu.HBM((rows, width * quarters), jnp.bfloat16),
        ],
        scratch_shapes=[
            pltpu.VMEM((quarters, rank, width), jnp.float32),
            pltpu.VMEM((quarters, rows, width), jnp.bfloat16),
            pltpu.VMEM((quarters - EARLY, rows, width), jnp.bfloat16),
            pltpu.SemaphoreType.DMA((2, quarters)),
            pltpu.SemaphoreType.DMA((quarters - EARLY,)),
        ],
        compiler_params=VMEM,
        name="feedback",
    )(total, *in_vmem(low_t, early), *in_hbm(late))


def local(layer_input, output_grad, feedback, basis_prev):
    early, late, tiles = corrected_and_factor(layer_input, output_grad, feedback, basis_prev)
    tiles = sum_all(tiles)
    factor_left, factor_low, terms = factor_and_terms(tiles, early, late, basis_prev.shape[0])

    block = jnp.sum(lax.all_to_all(terms, NEAR, 0, 0, tiled=True), 0)
    one, two, three = (shift(block, "zh", k) for k in (1, 2, 3))
    low_t = transposed_after(block, factor_low)
    block = (block + two) + (one + three)
    block, low_t = lax.optimization_barrier((block, low_t))
    basis_next, feedback_next = finish(copies(block, NEAR), low_t, early, late)
    return factor_left, basis_next, feedback_next


def solution(mesh):
    fine = Mesh(mesh.devices.reshape(4, 2, 4, 4, 2), ("zh", "zl", "x", "y", "c"))
    dp, tensor = ("zh", "zl", "x"), ("y", "c")
    in_specs = (P(dp, None), P(dp, tensor), P(dp, tensor), P(None, tensor))
    out_specs = (P(), P(None, tensor), P(dp, tensor))
    return jax.shard_map(local, mesh=fine, in_specs=in_specs, out_specs=out_specs, check_vma=False)
```

```python
import math

import jax
import jax.numpy as jnp
from jax import lax
from jax.experimental import pallas as pl
from jax.experimental.pallas import tpu as pltpu
from jax.sharding import Mesh
from jax.sharding import PartitionSpec as P

SIZES = dict(zh=4, zl=2, x=4, y=4, c=2)
PLANE = ("x", "y", "c")
LINE = ("zh", "zl")
NEAR = ("zl", "x")
REPLICAS = SIZES["zh"] * SIZES["zl"] * SIZES["x"]
QUARTERS = SIZES["x"]
HALVES = SIZES["zl"]
SPANS = 2
EARLY = 2
VMEM = pltpu.CompilerParams(vmem_limit_bytes=20 << 20)


def in_hbm(*arrays):
    return [pltpu.with_memory_space_constraint(a, pltpu.HBM) for a in arrays]


def in_vmem(*arrays):
    return [pltpu.with_memory_space_constraint(a, pltpu.VMEM) for a in arrays]


def shift(block, axis, step):
    n = SIZES[axis]
    return lax.ppermute(block, axis, [(i, (i + step) % n) for i in range(n)])


def copies(block, axes):
    n = math.prod(SIZES[a] for a in axes)
    sent = jnp.broadcast_to(block[None], (n,) + block.shape)
    return lax.all_to_all(sent, axes, 0, 0, tiled=True)


def sum_all(tiles):
    parts = lax.all_to_all(tiles, PLANE, 0, 0, tiled=True)
    parts = copies(jnp.sum(parts, 0), LINE)
    return copies(jnp.sum(parts, 0), PLANE)


def corrected_kernel(
    x_hbm, g_hbm, fb_hbm, basis_hbm, early_ref, late_hbm, tiles_ref,
    x_ref, g_ref, fb_ref, basis_ref, late_ref, x_sem, in_sems, out_sems,
):
    span = g_ref.shape[2]
    width = early_ref.shape[2]
    fetch_x = pltpu.make_async_copy(x_hbm, x_ref, x_sem)
    fetch_x.start()
    fetches = []
    for n in range(SPANS):
        columns = pl.ds(n * span, span)
        pairs = ((g_hbm, g_ref), (fb_hbm, fb_ref), (basis_hbm, basis_ref))
        fetches.append(
            [
                pltpu.make_async_copy(whole.at[:, columns], part.at[n], in_sems.at[n, i])
                for i, (whole, part) in enumerate(pairs)
            ]
        )
        for fetch in fetches[n]:
            fetch.start()
    fetch_x.wait()
    xt = x_ref[...].T
    parts = []
    stores = []
    for n in range(SPANS):
        for fetch in fetches[n]:
            fetch.wait()
        grad = jnp.dot(xt, g_ref[n], preferred_element_type=jnp.float32)
        grad = grad * (1.0 / math.sqrt(x_ref.shape[0])) + fb_ref[n].astype(jnp.float32)
        corrected = grad.astype(jnp.bfloat16)
        for i in range(span // width):
            q = n * (span // width) + i
            piece = corrected[:, i * width : (i + 1) * width]
            if q < EARLY:
                early_ref[q] = piece
            else:
                late = q - EARLY
                late_ref[late] = piece
                stores.append(pltpu.make_async_copy(late_ref.at[late], late_hbm.at[late], out_sems.at[late]))
                stores[-1].start()
        parts.append(
            lax.dot_general(
                basis_ref[n].astype(jnp.bfloat16),
                corrected,
                (((1,), (1,)), ((), ())),
                preferred_element_type=jnp.float32,
            )
        )
    total = sum(parts[1:], parts[0])
    rows, columns = total.shape
    for i in range(rows // 8):
        for j in range(columns // 128):
            tiles_ref[i * (columns // 128) + j] = total[8 * i : 8 * i + 8, 128 * j : 128 * j + 128]
    for store in stores:
        store.wait()


def corrected_and_factor(layer_input, output_grad, feedback, basis_prev):
    tokens, rows = layer_input.shape
    columns, rank = output_grad.shape[1], basis_prev.shape[0]
    width = columns // QUARTERS
    return pl.pallas_call(
        corrected_kernel,
        in_specs=[pl.BlockSpec(memory_space=pltpu.HBM)] * 4,
        out_specs=[pl.BlockSpec(memory_space=space) for space in (pltpu.VMEM, pltpu.HBM, pltpu.VMEM)],
        out_shape=[
            pltpu.VMEM((EARLY, rows, width), jnp.bfloat16),
            pltpu.HBM((QUARTERS - EARLY, rows, width), jnp.bfloat16),
            jax.ShapeDtypeStruct((rank * rows // 1024, 8, 128), jnp.float32),
        ],
        scratch_shapes=[
            pltpu.VMEM((tokens, rows), jnp.bfloat16),
            pltpu.VMEM((SPANS, tokens, columns // SPANS), jnp.bfloat16),
            pltpu.VMEM((SPANS, rows, columns // SPANS), jnp.bfloat16),
            pltpu.VMEM((SPANS, rank, columns // SPANS), jnp.float32),
            pltpu.VMEM((QUARTERS - EARLY, rows, width), jnp.bfloat16),
            pltpu.SemaphoreType.DMA(()),
            pltpu.SemaphoreType.DMA((SPANS, 3)),
            pltpu.SemaphoreType.DMA((QUARTERS - EARLY,)),
        ],
        compiler_params=VMEM,
        name="corrected",
    )(*in_hbm(layer_input, output_grad, feedback, basis_prev))


def eliminate(factor):
    rank, columns = factor.shape
    both = jnp.concatenate([factor, factor], 0)
    gram = lax.dot_general(
        factor,
        both,
        (((1,), (1,)), ((), ())),
        preferred_element_type=jnp.float32,
        precision=lax.Precision.HIGHEST,
    )
    blocks = rank // 8
    lanes = columns // 128
    table = [
        [gram[8 * i : 8 * i + 8]]
        + [factor[8 * i : 8 * i + 8, 128 * j : 128 * j + 128] for j in range(lanes)]
        for i in range(blocks)
    ]
    sublane = lax.broadcasted_iota(jnp.int32, (8, 128), 0)
    spread = lambda row: jnp.broadcast_to(row, (8, 128))
    out = []
    for p in range(blocks):
        below = range(p, blocks)
        col = [
            {i: jnp.broadcast_to(table[i][0][:, 8 * p + j : 8 * p + j + 1], (8, 128)) for i in below}
            for j in range(8)
        ]
        pivots = jnp.ones((8, 128), jnp.float32)
        for j in range(8):
            pivot = spread(col[j][p][j : j + 1])
            pivots = jnp.where(sublane == j, pivot, pivots)
            if p == blocks - 1 and j == 7:
                break
            inverse = 1.0 / pivot
            mult = {i: col[j][i] * inverse for i in below}
            mult[p] = jnp.where(sublane > j, mult[p], 0.0)
            for k in range(j + 1, 8):
                entry = spread(col[j][p][k : k + 1])
                for i in below:
                    col[k][i] = col[k][i] - mult[i] * entry
            for t in range(lanes + 1):
                if t == 0 and p == blocks - 1:
                    continue
                row = spread(table[p][t][j : j + 1])
                for i in below:
                    table[i][t] = table[i][t] - mult[i] * row
        scale = lax.rsqrt(pivots)
        out.append([table[p][t] * scale for t in range(1, lanes + 1)])
    return out


def factor_kernel(tiles_ref, early_ref, late_hbm, left_ref, low_ref, terms_ref, late_ref, sem):
    fetch = pltpu.make_async_copy(late_hbm, late_ref, sem)
    fetch.start()
    rank, columns = left_ref.shape
    lanes = columns // 128
    factor = jnp.concatenate(
        [
            jnp.concatenate([tiles_ref[i * lanes + j] for j in range(lanes)], 1)
            for i in range(rank // 8)
        ],
        0,
    )
    blocks = eliminate(factor)
    for i, block in enumerate(blocks):
        for j, tile in enumerate(block):
            left_ref[8 * i : 8 * i + 8, 128 * j : 128 * j + 128] = tile
    low = left_ref[...].astype(jnp.bfloat16)
    low_ref[...] = low
    for q in range(QUARTERS):
        if q == EARLY:
            fetch.wait()
        corrected = early_ref[q] if q < EARLY else late_ref[q - EARLY]
        term = jnp.dot(low, corrected, preferred_element_type=jnp.float32)
        for h in range(HALVES):
            terms_ref[h * QUARTERS + q] = term[h * (rank // HALVES) : (h + 1) * (rank // HALVES)]


def factor_and_terms(tiles, early, late, rank):
    _, rows, width = late.shape
    whole = pl.BlockSpec(memory_space=pltpu.VMEM)
    return pl.pallas_call(
        factor_kernel,
        in_specs=[whole, whole, pl.BlockSpec(memory_space=pltpu.HBM)],
        out_specs=[whole] * 3,
        out_shape=[
            jax.ShapeDtypeStruct((rank, rows), jnp.float32),
            jax.ShapeDtypeStruct((rank, rows), jnp.bfloat16),
            jax.ShapeDtypeStruct((HALVES * QUARTERS, rank // HALVES, width), jnp.float32),
        ],
        scratch_shapes=[pltpu.VMEM(late.shape, jnp.bfloat16), pltpu.SemaphoreType.DMA(())],
        compiler_params=VMEM,
        name="factor",
    )(tiles, *in_vmem(early), *in_hbm(late))


def transpose_kernel(after_ref, low_ref, low_t_ref):
    low_t_ref[...] = low_ref[...].astype(jnp.float32).T.astype(jnp.bfloat16)


def transposed_after(before, low):
    return pl.pallas_call(
        transpose_kernel,
        in_specs=[pl.BlockSpec(memory_space=pl.ANY), pl.BlockSpec(memory_space=pltpu.VMEM)],
        out_specs=pl.BlockSpec(memory_space=pltpu.VMEM),
        out_shape=pltpu.VMEM(low.shape[::-1], low.dtype),
        compiler_params=VMEM,
        name="transpose",
    )(before, low)


def feedback_kernel(
    total_ref, low_t_ref, early_ref, late_hbm, next_hbm, feedback_hbm, next_ref, out_ref, late_ref, sems, late_sems
):
    quarters, rows, width = out_ref.shape
    fetches = [
        pltpu.make_async_copy(late_hbm.at[i], late_ref.at[i], late_sems.at[i])
        for i in range(late_ref.shape[0])
    ]
    for fetch in fetches:
        fetch.start()
    stores = []
    for q in range(quarters):
        columns = pl.ds(q * width, width)
        basis_next = jnp.concatenate([total_ref[h * quarters + q] for h in range(HALVES)], 0) * (1.0 / REPLICAS)
        next_ref[q] = basis_next
        stores.append(pltpu.make_async_copy(next_ref.at[q], next_hbm.at[:, columns], sems.at[0, q]))
        stores[-1].start()
        approx = jnp.dot(
            low_t_ref[...], basis_next.astype(jnp.bfloat16), preferred_element_type=jnp.float32
        )
        if q >= EARLY:
            fetches[q - EARLY].wait()
        corrected = early_ref[q] if q < EARLY else late_ref[q - EARLY]
        out_ref[q] = (corrected.astype(jnp.float32) - approx).astype(jnp.bfloat16)
        stores.append(pltpu.make_async_copy(out_ref.at[q], feedback_hbm.at[:, columns], sems.at[1, q]))
        stores[-1].start()
    for store in stores:
        store.wait()


def finish(total, low_t, early, late):
    _, rows, width = late.shape
    quarters = QUARTERS
    rank = low_t.shape[1]
    hbm = pl.BlockSpec(memory_space=pltpu.HBM)
    whole = pl.BlockSpec(memory_space=pltpu.VMEM)
    return pl.pallas_call(
        feedback_kernel,
        in_specs=[whole, whole, whole, hbm],
        out_specs=[hbm, hbm],
        out_shape=[
            pltpu.HBM((rank, width * quarters), jnp.float32),
            pltpu.HBM((rows, width * quarters), jnp.bfloat16),
        ],
        scratch_shapes=[
            pltpu.VMEM((quarters, rank, width), jnp.float32),
            pltpu.VMEM((quarters, rows, width), jnp.bfloat16),
            pltpu.VMEM((quarters - EARLY, rows, width), jnp.bfloat16),
            pltpu.SemaphoreType.DMA((2, quarters)),
            pltpu.SemaphoreType.DMA((quarters - EARLY,)),
        ],
        compiler_params=VMEM,
        name="feedback",
    )(total, *in_vmem(low_t, early), *in_hbm(late))


def local(layer_input, output_grad, feedback, basis_prev):
    early, late, tiles = corrected_and_factor(layer_input, output_grad, feedback, basis_prev)
    tiles = sum_all(tiles)
    factor_left, factor_low, terms = factor_and_terms(tiles, early, late, basis_prev.shape[0])

    block = jnp.sum(lax.all_to_all(terms, NEAR, 0, 0, tiled=True), 0)
    one, two, three = (shift(block, "zh", k) for k in (1, 2, 3))
    low_t = transposed_after(block, factor_low)
    block = (block + two) + (one + three)
    block, low_t = lax.optimization_barrier((block, low_t))
    basis_next, feedback_next = finish(copies(block, NEAR), low_t, early, late)
    return factor_left, basis_next, feedback_next


def solution(mesh):
    fine = Mesh(mesh.devices.reshape(4, 2, 4, 4, 2), ("zh", "zl", "x", "y", "c"))
    dp, tensor = ("zh", "zl", "x"), ("y", "c")
    in_specs = (P(dp, None), P(dp, tensor), P(dp, tensor), P(None, tensor))
    out_specs = (P(), P(None, tensor), P(dp, tensor))
    return jax.shard_map(local, mesh=fine, in_specs=in_specs, out_specs=out_specs, check_vma=False)
```
